32 devices in a mesh: group: 2 (over y), ctx: 4 (over z), kvh: 2 (over x), sub: 2 (over core).
Axes of the slice: x: 2, y: 2, z: 4, core: 2. Of those that a mesh axis runs over, the one named last changes fastest.
Arguments:
- queries: bfloat16 [64, 128, 8192], P(('group', 'ctx'), 'sub', 'kvh'), parts along dimension 0, may hold values from -128 to 128
- cache_kv: bfloat16 [192, 128, 2048], P(('group', 'ctx'), None, 'kvh'), parts along dimension 0, may hold values from -4 to 4
- cache_scale: float32 [192, 16], P('group', 'kvh'), parts along dimension 0, may hold values from 0.29 to 3.01
- prompt_key_value: bfloat16 [64, 128, 2048], P(('group', 'ctx'), None, 'kvh'), parts along dimension 0, may hold values from -4 to 4
- prompt_scale: float32 [64, 16], P('group', 'kvh'), parts along dimension 0, may hold values from 0.3 to 3
- rand_blocks: int32 [64, 3], P('group'), parts along dimension 0, may hold values from 0 to 95, as said below
Outputs:
- attended: bfloat16 [64, 128, 8192], P(('group', 'ctx'), 'sub', 'kvh'), parts along dimension 0
The draws below stay inside these ranges and needn't reach their ends.
There are 2 independent parts, one for each index of `group`. The reference program is written for one: setup_inputs(seed, part) draws one part's arguments, and reference() takes and returns one part's arrays. A program takes and returns all parts, laid end to end along the dimension named above; each array names one. Nothing has to cross between parts.
Inputs may be any that keep to these rules, and one draw needn't show every extreme that they name: `rand_blocks`: within each aligned run of 8 prompt blocks, the run's entries name blocks of any one aligned range of 24 cache blocks at most 6 times; one and the same range is named exactly 6 times in every run, and each run has another range so named.
All inputs are finite; a program needn't handle non-finite values.
Results may differ from the reference program's by a relative error of at most 0.0051.
Values may be sent and summed in bfloat16 or wider, within the bound.
A program may use at most 64 MiB of HBM per device.

```python
import math
import jax
import jax.numpy as jnp
from jax import lax

QUERY_HEADS = 64
KEY_VALUE_HEADS = 8
HEAD_SIZE = 128
BLOCK_TOKENS = 128
NG = 2
R = 3
WIN = 2
QB_DEV = 8
NB_DEV = 24
PROMPT_BLOCKS = 32
CACHE_BLOCK_COUNT = 96
CAP = 6
N_CTX = 4


def shared_tables(key):
    base = jax.random.fold_in(key, 11)
    key_scale_rows = jax.random.fold_in(base, 1)
    scale_factors = jnp.exp(jax.random.uniform(key_scale_rows, (CACHE_BLOCK_COUNT, 2 * KEY_VALUE_HEADS), jnp.float32, math.log(0.3), math.log(3.0)))
    return scale_factors


def draw_cache_scale(key, part):
    return shared_tables(key).astype(jnp.float32)


def draw_cache_kv(key, part):
    base = jax.random.fold_in(key, 23)
    array_shape = (CACHE_BLOCK_COUNT, BLOCK_TOKENS, KEY_VALUE_HEADS, 2, HEAD_SIZE)
    value_rows = jnp.clip(jax.random.normal(base, array_shape, jnp.float32), -4.0, 4.0)
    return value_rows.reshape(CACHE_BLOCK_COUNT, BLOCK_TOKENS, KEY_VALUE_HEADS * 2 * HEAD_SIZE).astype(jnp.bfloat16)


def draw_queries(key, part):
    base = jax.random.fold_in(key, 37)
    key_vals = jax.random.fold_in(base, 0)
    query_groups = QUERY_HEADS // KEY_VALUE_HEADS
    array_shape = (PROMPT_BLOCKS, BLOCK_TOKENS, KEY_VALUE_HEADS, query_groups, HEAD_SIZE)
    value_rows = jnp.clip(1.5 * jax.random.normal(key_vals, array_shape, jnp.float32), -6.0, 6.0)
    return value_rows.reshape(PROMPT_BLOCKS, BLOCK_TOKENS, QUERY_HEADS * HEAD_SIZE).astype(jnp.bfloat16)


def draw_rand_blocks(key, part):
    need = QB_DEV * R
    slot_total = N_CTX * CAP
    keys = jax.random.split(jax.random.fold_in(key, 41), 5)
    star = jax.random.randint(keys[0], (), 0, N_CTX)
    second = (star + 1 + jax.random.randint(keys[1], (N_CTX, 1), 0, N_CTX - 1)) % N_CTX
    slot_owner = (jnp.arange(slot_total, dtype=jnp.int32) // CAP)[None, :]
    forced = ((slot_owner == star) | (slot_owner == second)).astype(jnp.int32)
    noise = jax.random.randint(keys[2], (N_CTX, slot_total), 0, 1 << 16)
    priority = forced * (1 << 28) + noise * slot_total + jnp.arange(slot_total, dtype=jnp.int32)[None, :]
    order = jnp.argsort(-priority, axis=1, stable=True)[:, :need]
    chosen = order // CAP
    shuffle_noise = jax.random.randint(keys[3], (N_CTX, need), 0, 1 << 16) * need + jnp.arange(need, dtype=jnp.int32)[None, :]
    shuffle = jnp.argsort(shuffle_noise, axis=1, stable=True)
    chosen = jnp.take_along_axis(chosen, shuffle, axis=1)
    local = jax.random.randint(keys[4], (N_CTX, need), 0, NB_DEV)
    return (chosen * NB_DEV + local).reshape(N_CTX * QB_DEV, R).astype(jnp.int32)


def block_scale(rng, extent, pieces, least, largest):
    gain, own = 1.0, jax.random.fold_in(rng, 6)
    for axis_at, blocks in pieces:
        steps = jnp.exp(jax.random.uniform(jax.random.fold_in(own, axis_at), (blocks,), jnp.float32, least / len(pieces), largest / len(pieces)))
        gain = gain * jnp.repeat(steps, extent[axis_at] // blocks).reshape([-1 if axis == axis_at else 1 for axis in range(len(extent))])
    return gain


def scatter_about(stream_key, shape, deviation, reach, pieces=(), kind=jnp.bfloat16):
    gain = block_scale(stream_key, shape, pieces, -0.22, 0.18) if pieces else 1.0
    array = jax.random.normal(stream_key, shape, jnp.float32) * deviation * gain
    return jnp.minimum(jnp.maximum(array, -reach), reach).astype(kind)


def setup_inputs(seed: int = 0, part: int = 0) -> dict:
    arg_keys = jax.random.split(jax.random.key(seed), 7)
    own_keys = jax.random.split(jax.random.fold_in(arg_keys[6], part), 7)
    queries = draw_queries(jax.random.fold_in(jax.random.fold_in(arg_keys[6], part), 71), part)
    cache_kv = draw_cache_kv(jax.random.fold_in(jax.random.fold_in(arg_keys[6], part), 71), part)
    cache_scale = draw_cache_scale(jax.random.fold_in(jax.random.fold_in(arg_keys[6], part), 71), part)
    prompt_key_value = scatter_about(own_keys[3], (PROMPT_BLOCKS, BLOCK_TOKENS, KEY_VALUE_HEADS * 2 * HEAD_SIZE), 1.0, 4.0, ((0, 4), (2, 2)))
    prompt_scale = jnp.clip(jnp.exp(math.log(3.0) - 2.3025851 * jax.random.uniform(own_keys[4], (PROMPT_BLOCKS, KEY_VALUE_HEADS * 2), jnp.float32) ** block_scale(own_keys[4], (PROMPT_BLOCKS, KEY_VALUE_HEADS * 2), ((1, 2),), -0.2, 0.2)), 0.3, 3.0)
    rand_blocks = draw_rand_blocks(jax.random.fold_in(jax.random.fold_in(arg_keys[6], part), 71), part)
    return {"queries": queries, "cache_kv": cache_kv, "cache_scale": cache_scale, "prompt_key_value": prompt_key_value, "prompt_scale": prompt_scale, "rand_blocks": rand_blocks}


def reference(queries, cache_kv, cache_scale, prompt_key_value, prompt_scale, rand_blocks):
    query_groups = QUERY_HEADS // KEY_VALUE_HEADS
    key_total = NG + R + WIN + 1
    steps_back = jnp.arange(WIN, 0, -1, dtype=jnp.int32)
    row_ids = jnp.arange(BLOCK_TOKENS, dtype=jnp.int32)
    key_ids = jnp.arange(key_total * BLOCK_TOKENS, dtype=jnp.int32)
    last_start = (key_total - 1) * BLOCK_TOKENS

    def one_block(block_number):
        cache_ids = jnp.concatenate([jnp.arange(NG, dtype=jnp.int32), rand_blocks[block_number].astype(jnp.int32)])
        back_ids = block_number - steps_back
        prompt_ids = jnp.concatenate([jnp.maximum(back_ids, 0), jnp.reshape(block_number, (1,))]).astype(jnp.int32)
        prompt_ok = jnp.concatenate([back_ids >= 0, jnp.ones((1,), dtype=bool)])
        block_ok = jnp.concatenate([jnp.ones((NG + R,), dtype=bool), prompt_ok])
        collected_rows = jnp.concatenate([cache_kv[cache_ids], prompt_key_value[prompt_ids]], axis=0)
        scale_row_table = jnp.concatenate([cache_scale[cache_ids], prompt_scale[prompt_ids]], axis=0)
        collected_rows = collected_rows.reshape(key_total * BLOCK_TOKENS, KEY_VALUE_HEADS, 2, HEAD_SIZE)
        key_vals = collected_rows[:, :, 0].astype(jnp.float32)
        value_vals = collected_rows[:, :, 1].astype(jnp.float32)
        scale_row_table = scale_row_table.reshape(key_total, KEY_VALUE_HEADS, 2)
        key_scale = jnp.repeat(scale_row_table[:, :, 0], BLOCK_TOKENS, axis=0).T
        value_scale = jnp.repeat(scale_row_table[:, :, 1], BLOCK_TOKENS, axis=0).T
        query_entries = queries[block_number].reshape(BLOCK_TOKENS, KEY_VALUE_HEADS, query_groups, HEAD_SIZE).astype(jnp.float32)
        scores = jnp.einsum('rhgd,khd->hgrk', query_entries, key_vals)
        scores = scores * (key_scale / math.sqrt(HEAD_SIZE))[:, None, None, :]
        causal = (key_ids[None, :] < last_start) | (key_ids[None, :] - last_start <= row_ids[:, None])
        allowed = causal & jnp.repeat(block_ok, BLOCK_TOKENS)[None, :]
        scores = jnp.where(allowed[None, None], scores, -jnp.inf)
        row_max = lax.optimization_barrier(jnp.max(scores, axis=-1, keepdims=True))
        probs = jnp.exp(scores - row_max)
        totals = lax.optimization_barrier(jnp.sum(probs, axis=-1))
        weights = (probs * value_scale[:, None, None, :]).astype(jnp.bfloat16)
        result = jnp.einsum('hgrk,khd->rhgd', weights.astype(jnp.float32), value_vals)
        result = result / jnp.transpose(totals, (2, 0, 1))[..., None]
        return result.astype(jnp.bfloat16).reshape(BLOCK_TOKENS, QUERY_HEADS * HEAD_SIZE)
    return lax.map(one_block, jnp.arange(PROMPT_BLOCKS, dtype=jnp.int32))
```

```python
import functools
import math

import jax
import jax.numpy as jnp
from jax import lax
from jax.experimental import pallas as pl
from jax.experimental.pallas import tpu as pltpu
from jax.sharding import PartitionSpec as P

HEAD = 128
NG = 2
WIN = 2
FAR = -1e30
MESH = pl.DeviceIdType.MESH


def flipped(me, k):
    out, bit = me, 1
    while bit <= k:
        if k & bit:
            out = out + bit - 2 * bit * ((me // bit) % 2)
        bit *= 2
    return out


def kernel(
    n, cap, q_hbm, c_hbm, cs, p_hbm, ps, rnd, o_hbm,
    qbuf, cbuf, pk, gbuf, pool, outb, obuf, acc1, m1, l1, bias, places,
    loc, osem, rs, rr, fs, fr, gs, gr, gfs, gfr, ws, wr, wfs, wfr,
):
    nq, rows, width = q_hbm.shape
    nc, block, kvw = c_hbm.shape
    heads = kvw // (2 * HEAD)
    groups = width // (heads * HEAD)
    lanes = groups * rows
    half = block // 2
    rand = rnd.shape[1]
    me, sub = lax.axis_index("ctx"), lax.axis_index("sub")
    other = 1 - sub
    mine = pl.ds(pl.multiple_of(sub * half, half), half)
    theirs = pl.ds(pl.multiple_of(other * half, half), half)
    order = range(n - 1, 0, -1)

    local_p = pltpu.make_async_copy(p_hbm, pk.at[pl.ds(WIN, nq)], loc.at[0])
    local_c = pltpu.make_async_copy(c_hbm, cbuf, loc.at[1])
    local_q = pltpu.make_async_copy(q_hbm, qbuf, loc.at[2])
    local_g = pltpu.make_async_copy(c_hbm.at[pl.ds(0, NG)], gbuf, loc.at[3])

    @pl.when(me == 0)
    def _():
        local_g.start()

    local_p.start()
    local_c.start()
    local_q.start()

    barrier = pltpu.get_barrier_semaphore()
    for k in order:
        pl.semaphore_signal(barrier, inc=1, device_id={"ctx": flipped(me, k)}, device_id_type=MESH)
    pl.semaphore_signal(barrier, inc=1, device_id={"sub": other}, device_id_type=MESH)
    pl.semaphore_wait(barrier, n)

    def remote(src, dst, send, recv, where):
        return pltpu.make_async_remote_copy(
            src_ref=src, dst_ref=dst, send_sem=send, recv_sem=recv,
            device_id=where, device_id_type=MESH,
        )

    onward = {"ctx": lax.rem(me + 1, n)}
    sibling = {"sub": other}
    send_g = remote(gbuf.at[:, mine], gbuf.at[:, mine], gs, gr, onward)
    share_g = remote(gbuf.at[:, mine], gbuf.at[:, mine], gfs, gfr, sibling)
    heard_g = remote(gbuf.at[:, theirs], gbuf.at[:, theirs], gfs, gfr, sibling)
    send_w = remote(pk.at[pl.ds(nq, WIN), mine], pk.at[pl.ds(0, WIN), mine], ws, wr, onward)
    share_w = remote(pk.at[pl.ds(0, WIN), mine], pk.at[pl.ds(0, WIN), mine], wfs, wfr, sibling)
    heard_w = remote(pk.at[pl.ds(0, WIN), theirs], pk.at[pl.ds(0, WIN), theirs], wfs, wfr, sibling)

    def run(owner, side):
        return pool.at[pl.ds((owner * 2 + side) * cap, cap)]

    def send_r(k):
        return remote(outb.at[k - 1], run(me, sub), rs.at[k - 1], rr.at[k - 1], {"ctx": flipped(me, k)})

    def came_r(k):
        mate = flipped(me, k)
        return remote(outb.at[k - 1], run(mate, sub), rs.at[k - 1], rr.at[k - 1], {"ctx": mate})

    def share_r(k):
        part = run(flipped(me, k), sub)
        return remote(part, part, fs.at[k - 1], fr.at[k - 1], sibling)

    def heard_r(k):
        part = run(flipped(me, k), other)
        return remote(part, part, fs.at[k - 1], fr.at[k - 1], sibling)

    @pl.when(me == 0)
    def _():
        local_g.wait()
        send_g.start()

    local_p.wait()

    @pl.when(me < n - 1)
    def _():
        send_w.start()

    local_c.wait()

    def picks(reader):
        def step(b, carry):
            count, slots = carry[0], list(carry[1:])
            for r in range(rand):
                ref = rnd[reader * nq + b, r]
                own = lax.div(ref, nc) == me
                for j in range(cap):
                    slots[j] = jnp.where(own & (count == j), ref - me * nc, slots[j])
                count = count + own.astype(jnp.int32)
            return (count, *slots)

        zero = jnp.int32(0)
        return lax.fori_loop(0, nq, step, (zero,) * (cap + 1))[1:]

    for k in order:
        for j, slot in enumerate(picks(flipped(me, k))):
            outb[k - 1, j] = cbuf[slot, mine, :]
        send_r(k).start()
    for j, slot in enumerate(picks(me)):
        for side in range(2):
            pool[(me * 2 + side) * cap + j] = cbuf[slot, pl.ds(side * half, half), :]

    def place(i, _):
        ref = rnd[me * nq + i // rand, i % rand]
        owner = lax.div(ref, nc)

        def earlier(j, count):
            same = lax.div(rnd[me * nq + j // rand, j % rand], nc) == owner
            return count + same.astype(jnp.int32)

        places[i] = owner * (2 * cap) + lax.fori_loop(0, i, earlier, jnp.int32(0))
        return 0

    lax.fori_loop(0, nq * rand, place, 0)
    key_row = lax.broadcasted_iota(jnp.int32, (block, lanes), 0)
    query_row = lax.broadcasted_iota(jnp.int32, (block, lanes), 1) % rows + sub * rows
    bias[...] = jnp.where(key_row <= query_row, 0.0, FAR).astype(jnp.float32)

    @pl.when(me > 0)
    def _():
        send_g.wait_recv()
        share_g.start()

        @pl.when(me < n - 1)
        def _():
            send_g.start()

        send_w.wait_recv()
        share_w.start()
        heard_g.wait_recv()
        heard_w.wait_recv()

    @pl.when(me == 0)
    def _():
        pk[pl.ds(0, WIN)] = jnp.zeros((WIN, block, kvw), pk.dtype)

    local_q.wait()
    unit = math.log2(math.e) / math.sqrt(HEAD)

    def head_queries(b, h):
        at = h * groups * HEAD
        return jnp.concatenate(
            [qbuf[b, :, at + g * HEAD : at + (g + 1) * HEAD] for g in range(groups)], axis=0
        )

    def columns(h, value):
        return slice((2 * h + value) * HEAD, (2 * h + value + 1) * HEAD)

    def part(q, keys, values, scales, masked, carry):
        st = lax.dot_general(
            jnp.concatenate(keys, axis=0), q, (((1,), (1,)), ((), ())),
            preferred_element_type=jnp.float32,
        )
        pieces = [st[j * block : (j + 1) * block] for j in range(len(scales))]
        if masked:
            pieces[-1] = pieces[-1] + bias[...]
        tops = [
            jnp.max(piece, axis=0, keepdims=True) * c + off
            for piece, (c, _, off) in zip(pieces, scales)
        ]
        top = functools.reduce(jnp.maximum, tops)
        if carry is not None:
            top = jnp.maximum(top, carry[0])
        total, weights = 0.0, []
        for piece, (c, v, off) in zip(pieces, scales):
            v = jnp.full((1, lanes), v, jnp.float32)
            w = jnp.exp2(piece * c - (top - off - jnp.log2(v)))
            total = total + jnp.sum(w, axis=0, keepdims=True) / v
            weights.append(w.astype(jnp.bfloat16))
        acc = lax.dot_general(
            jnp.concatenate(values, axis=0), jnp.concatenate(weights, axis=0),
            (((0,), (0,)), ((), ())), preferred_element_type=jnp.float32,
        )
        if carry is not None:
            fade = jnp.exp2(carry[0] - top)
            total = total + carry[1] * fade
            acc = acc + carry[2] * fade
        return top, total, acc

    def near(b, _):
        at = me * nq + b
        for h in range(heads):
            q = head_queries(b, h)
            keys, values = [], []
            for value, into in ((0, keys), (1, values)):
                cols = columns(h, value)
                into += [gbuf[j, :, cols] for j in range(NG)]
                into += [pk[b + j, :, cols] for j in range(WIN + 1)]
            scales = [(cs[j, 2 * h] * unit, cs[j, 2 * h + 1], 0.0) for j in range(NG)]
            for j in range(WIN, 0, -1):
                there = at >= j
                row = jnp.maximum(at - j, 0)
                c = jnp.where(there, ps[row, 2 * h] * unit, 0.0)
                scales.append((c, ps[row, 2 * h + 1], jnp.where(there, 0.0, FAR)))
            scales.append((ps[at, 2 * h] * unit, ps[at, 2 * h + 1], 0.0))
            m1[b, h], l1[b, h], acc1[b, h] = part(q, keys, values, scales, True, None)
        return 0

    lax.fori_loop(0, nq, near, 0)

    for k in reversed(order):
        came_r(k).wait_recv()
        share_r(k).start()
    for k in order:
        heard_r(k).wait_recv()

    def far(b, _):
        spots = [places[b * rand + r] for r in range(rand)]
        refs = [rnd[me * nq + b, r] for r in range(rand)]
        for h in range(heads):
            q = head_queries(b, h)
            keys, values = [], []
            for value, into in ((0, keys), (1, values)):
                cols = columns(h, value)
                for spot in spots:
                    into += [pool[spot, :, cols], pool[spot + cap, :, cols]]
            scales = [(cs[ref, 2 * h] * unit, cs[ref, 2 * h + 1], 0.0) for ref in refs]
            carry = (m1[b, h], l1[b, h], acc1[b, h])
            _, total, acc = part(q, keys, values, scales, False, carry)
            out = jnp.transpose(acc / total).astype(jnp.bfloat16)
            at = h * groups * HEAD
            for g in range(groups):
                obuf[b, :, at + g * HEAD : at + (g + 1) * HEAD] = out[g * rows : (g + 1) * rows]
        pltpu.make_async_copy(obuf.at[b], o_hbm.at[b], osem.at[b]).start()
        return 0

    lax.fori_loop(0, nq, far, 0)

    for b in range(nq):
        pltpu.make_async_copy(obuf.at[b], o_hbm.at[b], osem.at[b]).wait()

    @pl.when(me < n - 1)
    def _():
        send_g.wait_send()
        send_w.wait_send()

    @pl.when(me > 0)
    def _():
        share_g.wait_send()
        share_w.wait_send()

    for k in order:
        send_r(k).wait_send()
        share_r(k).wait_send()


def body(queries, cache_kv, cache_scale, prompt_key_value, prompt_scale, rand_blocks):
    n = lax.axis_size("ctx")
    nq, rows, width = queries.shape
    nc, block, kvw = cache_kv.shape
    rand = rand_blocks.shape[1]
    cap = max(2, (nq * rand + n - 1) // n)
    heads = kvw // (2 * HEAD)
    lanes = width // (heads * HEAD) * rows
    half = block // 2
    bf, f32 = jnp.bfloat16, jnp.float32
    hbm = pl.BlockSpec(memory_space=pl.ANY)
    smem = pl.BlockSpec(memory_space=pltpu.SMEM)
    dma = pltpu.SemaphoreType.DMA
    keys = (NG + rand + WIN + 1) * block
    return pl.pallas_call(
        functools.partial(kernel, n, cap),
        out_shape=jax.ShapeDtypeStruct(queries.shape, bf),
        in_specs=[hbm, hbm, smem, hbm, smem, smem],
        out_specs=hbm,
        scratch_shapes=[
            pltpu.VMEM((nq, rows, width), bf),
            pltpu.VMEM((nc, block, kvw), bf),
            pltpu.VMEM((WIN + nq, block, kvw), bf),
            pltpu.VMEM((NG, block, kvw), bf),
            pltpu.VMEM((n * 2 * cap, half, kvw), bf),
            pltpu.VMEM((n - 1, cap, half, kvw), bf),
            pltpu.VMEM((nq, rows, width), bf),
            pltpu.VMEM((nq, heads, HEAD, lanes), f32),
            pltpu.VMEM((nq, heads, 1, lanes), f32),
            pltpu.VMEM((nq, heads, 1, lanes), f32),
            pltpu.VMEM((block, lanes), f32),
            pltpu.SMEM((nq * rand,), jnp.int32),
            dma((4,)), dma((nq,)),
            dma((n - 1,)), dma((n - 1,)), dma((n - 1,)), dma((n - 1,)),
            dma, dma, dma, dma, dma, dma, dma, dma,
        ],
        compiler_params=pltpu.CompilerParams(
            collective_id=0, has_side_effects=True, vmem_limit_bytes=56 * 2**20
        ),
        cost_estimate=pl.CostEstimate(
            flops=4 * nq * width * rows * keys,
            bytes_accessed=2 * nc * block * kvw + 4 * nq * rows * width,
            transcendentals=nq * heads * lanes * keys,
        ),
    )(queries, cache_kv, cache_scale, prompt_key_value, prompt_scale, rand_blocks)


def solution(mesh):
    in_specs = (
        P(("group", "ctx"), "sub", "kvh"),
        P(("group", "ctx"), None, "kvh"),
        P("group", "kvh"),
        P(("group", "ctx"), None, "kvh"),
        P("group", "kvh"),
        P("group", None),
    )
    out_specs = P(("group", "ctx"), "sub", "kvh")
    return jax.shard_map(body, mesh=mesh, in_specs=in_specs, out_specs=out_specs, check_vma=False)
```

```python
import functools
import math

import jax
import jax.numpy as jnp
from jax import lax
from jax.experimental import pallas as pl
from jax.experimental.pallas import tpu as pltpu
from jax.sharding import PartitionSpec as P

HEAD = 128
NG = 2
WIN = 2
FAR = -1e30
MESH = pl.DeviceIdType.MESH


def flipped(me, k):
    out, bit = me, 1
    while bit <= k:
        if k & bit:
            out = out + bit - 2 * bit * ((me // bit) % 2)
        bit *= 2
    return out


def kernel(
    n, cap, q_hbm, c_hbm, cs_hbm, p_hbm, ps_hbm, rnd_hbm, o_hbm,
    qbuf, cbuf, pk, gbuf, pools, outb, obuf, acc1, m1, l1, bias, places, cs, ps, rnd,
    loc, osem, rs, rr, fs, fr, gs, gr, gfs, gfr, ws, wr, wfs, wfr,
):
    nq, rows, width = q_hbm.shape
    nc, block, kvw = c_hbm.shape
    heads = kvw // (2 * HEAD)
    groups = width // (heads * HEAD)
    lanes = groups * rows
    half = block // 2
    rand = rnd.shape[0]
    pair = 2 * HEAD
    middle = n // 2
    me, sub = lax.axis_index("ctx"), lax.axis_index("sub")
    other = 1 - sub
    mine = pl.ds(pl.multiple_of(sub * half, half), half)
    theirs = pl.ds(pl.multiple_of(other * half, half), half)
    order = range(n - 1, 0, -1)

    local_p = pltpu.make_async_copy(p_hbm, pk.at[pl.ds(WIN, nq)], loc.at[0])
    local_c = pltpu.make_async_copy(c_hbm, cbuf, loc.at[1])
    local_q = pltpu.make_async_copy(q_hbm, qbuf, loc.at[2])
    local_g = pltpu.make_async_copy(c_hbm.at[pl.ds(0, NG)], gbuf, loc.at[3])

    @pl.when(me == 0)
    def _():
        local_g.start()

    local_p.start()
    local_c.start()
    tables = [
        pltpu.make_async_copy(a, b, loc.at[4 + i])
        for i, (a, b) in enumerate(((rnd_hbm, rnd), (cs_hbm, cs), (ps_hbm, ps)))
    ]
    for table in tables:
        table.start()

    barrier = pltpu.get_barrier_semaphore()
    for k in order:
        pl.semaphore_signal(barrier, inc=1, device_id={"ctx": flipped(me, k)}, device_id_type=MESH)
    pl.semaphore_signal(barrier, inc=1, device_id={"sub": other}, device_id_type=MESH)
    pl.semaphore_wait(barrier, n)

    def remote(src, dst, send, recv, where):
        return pltpu.make_async_remote_copy(
            src_ref=src, dst_ref=dst, send_sem=send, recv_sem=recv,
            device_id=where, device_id_type=MESH,
        )

    onward = {"ctx": lax.rem(me + 1, n)}
    across = {"ctx": lax.rem(me + middle, n)}
    sibling = {"sub": other}
    send_g = remote(gbuf.at[:, mine], gbuf.at[:, mine], gs.at[0], gr, onward)
    jump_g = remote(gbuf.at[:, mine], gbuf.at[:, mine], gs.at[1], gr, across)
    share_g = remote(gbuf.at[:, mine], gbuf.at[:, mine], gfs, gfr, sibling)
    heard_g = remote(gbuf.at[:, theirs], gbuf.at[:, theirs], gfs, gfr, sibling)
    send_w = remote(pk.at[pl.ds(nq, WIN), mine], pk.at[pl.ds(0, WIN), mine], ws, wr, onward)
    share_w = remote(pk.at[pl.ds(0, WIN), mine], pk.at[pl.ds(0, WIN), mine], wfs, wfr, sibling)
    heard_w = remote(pk.at[pl.ds(0, WIN), theirs], pk.at[pl.ds(0, WIN), theirs], wfs, wfr, sibling)

    def run(h, owner, side):
        return pools[h].at[pl.ds((owner * 2 + side) * cap, cap)]

    def send_r(k, h):
        at, mate = (k - 1, h), flipped(me, k)
        return remote(outb.at[at], run(h, me, sub), rs.at[at], rr.at[at], {"ctx": mate})

    def came_r(k, h):
        at, mate = (k - 1, h), flipped(me, k)
        return remote(outb.at[at], run(h, mate, sub), rs.at[at], rr.at[at], {"ctx": mate})

    def share_r(k, h):
        at, part = (k - 1, h), run(h, flipped(me, k), sub)
        return remote(part, part, fs.at[at], fr.at[at], sibling)

    def heard_r(k, h):
        at, part = (k - 1, h), run(h, flipped(me, k), other)
        return remote(part, part, fs.at[at], fr.at[at], sibling)

    passes = (me > 0) & (me + 1 < n) & (lax.rem(me + 1, n) != middle)

    @pl.when(me == 0)
    def _():
        local_g.wait()
        jump_g.start()
        if middle > 1:
            send_g.start()

    local_p.wait()

    @pl.when(me < n - 1)
    def _():
        send_w.start()

    local_c.wait()
    local_q.start()
    for table in tables:
        table.wait()

    def picks(reader):
        def step(b, carry):
            count, slots = carry[0], list(carry[1:])
            for r in range(rand):
                ref = rnd[r, reader * nq + b]
                own = lax.div(ref, nc) == me
                for j in range(cap):
                    slots[j] = jnp.where(own & (count == j), ref - me * nc, slots[j])
                count = count + own.astype(jnp.int32)
            return (count, *slots)

        zero = jnp.int32(0)
        return lax.fori_loop(0, nq, step, (zero,) * (cap + 1))[1:]

    for k in order:
        for j, slot in enumerate(picks(flipped(me, k))):
            for h in range(heads):
                outb[k - 1, h, j] = cbuf[slot, mine, h * pair : (h + 1) * pair]
        send_r(k, 0).start()
    if heads > 1:
        for k in order:
            send_r(k, 1).start()
    for j, slot in enumerate(picks(me)):
        for side in range(2):
            for h in range(heads):
                pools[h][(me * 2 + side) * cap + j] = cbuf[
                    slot, pl.ds(side * half, half), h * pair : (h + 1) * pair
                ]

    def place(i, _):
        ref = rnd[i % rand, me * nq + i // rand]
        owner = lax.div(ref, nc)

        def earlier(j, count):
            same = lax.div(rnd[j % rand, me * nq + j // rand], nc) == owner
            return count + same.astype(jnp.int32)

        places[i] = owner * (2 * cap) + lax.fori_loop(0, i, earlier, jnp.int32(0))
        return 0

    lax.fori_loop(0, nq * rand, place, 0)
    key_row = lax.broadcasted_iota(jnp.int32, (block, lanes), 0)
    query_row = lax.broadcasted_iota(jnp.int32, (block, lanes), 1) % rows + sub * rows
    bias[...] = jnp.where(key_row <= query_row, 0.0, FAR).astype(jnp.float32)

    @pl.when(me > 0)
    def _():
        send_g.wait_recv()

    @pl.when(passes)
    def _():
        send_g.start()

    @pl.when(me > 0)
    def _():
        share_g.start()
        send_w.wait_recv()
        share_w.start()

    for h in range(2, heads):
        for k in order:
            send_r(k, h).start()

    @pl.when(me > 0)
    def _():
        heard_g.wait_recv()
        heard_w.wait_recv()

    @pl.when(me == 0)
    def _():
        pk[pl.ds(0, WIN)] = jnp.zeros((WIN, block, kvw), pk.dtype)

    local_q.wait()
    unit = math.log2(math.e) / math.sqrt(HEAD)

    def head_queries(b, h):
        at = h * groups * HEAD
        return jnp.concatenate(
            [qbuf[b, :, at + g * HEAD : at + (g + 1) * HEAD] for g in range(groups)], axis=0
        )

    def columns(h, value):
        return slice((2 * h + value) * HEAD, (2 * h + value + 1) * HEAD)

    def part(q, keys, values, scales, masked, carry):
        st = lax.dot_general(
            jnp.concatenate(keys, axis=0), q, (((1,), (1,)), ((), ())),
            preferred_element_type=jnp.float32,
        )
        pieces = [st[j * block : (j + 1) * block] for j in range(len(scales))]
        if masked:
            pieces[-1] = pieces[-1] + bias[...]
        tops = [
            jnp.max(piece, axis=0, keepdims=True) * c + off
            for piece, (c, _, off) in zip(pieces, scales)
        ]
        top = functools.reduce(jnp.maximum, tops)
        if carry is not None:
            top = jnp.maximum(top, carry[0])
        total, weights = 0.0, []
        for piece, (c, v, off) in zip(pieces, scales):
            v = jnp.full((1, lanes), v, jnp.float32)
            w = jnp.exp2(piece * c - (top - off - jnp.log2(v)))
            total = total + jnp.sum(w, axis=0, keepdims=True) / v
            weights.append(w.astype(jnp.bfloat16))
        acc = lax.dot_general(
            jnp.concatenate(values, axis=0), jnp.concatenate(weights, axis=0),
            (((0,), (0,)), ((), ())), preferred_element_type=jnp.float32,
        )
        if carry is not None:
            fade = jnp.exp2(carry[0] - top)
            total = total + carry[1] * fade
            acc = acc + carry[2] * fade
        return top, total, acc

    def near(b, _):
        at = me * nq + b
        for h in range(heads):
            q = head_queries(b, h)
            keys, values = [], []
            for value, into in ((0, keys), (1, values)):
                cols = columns(h, value)
                into += [gbuf[j, :, cols] for j in range(NG)]
                into += [pk[b + j, :, cols] for j in range(WIN + 1)]
            scales = [(cs[2 * h, j] * unit, cs[2 * h + 1, j], 0.0) for j in range(NG)]
            for j in range(WIN, 0, -1):
                there = at >= j
                row = jnp.maximum(at - j, 0)
                c = jnp.where(there, ps[2 * h, row] * unit, 0.0)
                scales.append((c, ps[2 * h + 1, row], jnp.where(there, 0.0, FAR)))
            scales.append((ps[2 * h, at] * unit, ps[2 * h + 1, at], 0.0))
            m1[b, h], l1[b, h], acc1[b, h] = part(q, keys, values, scales, True, None)
        return 0

    lax.fori_loop(0, nq, near, 0)

    def far(h, b):
        spots = [places[b * rand + r] for r in range(rand)]
        refs = [rnd[r, me * nq + b] for r in range(rand)]
        q = head_queries(b, h)
        keys, values = [], []
        for value, into in ((0, keys), (1, values)):
            cols = slice(value * HEAD, (value + 1) * HEAD)
            for spot in spots:
                into += [pools[h][spot, :, cols], pools[h][spot + cap, :, cols]]
        scales = [(cs[2 * h, ref] * unit, cs[2 * h + 1, ref], 0.0) for ref in refs]
        carry = (m1[b, h], l1[b, h], acc1[b, h])
        _, total, acc = part(q, keys, values, scales, False, carry)
        out = jnp.transpose(acc / total).astype(jnp.bfloat16)
        at = h * groups * HEAD
        for g in range(groups):
            obuf[b, :, at + g * HEAD : at + (g + 1) * HEAD] = out[g * rows : (g + 1) * rows]

    span = groups * HEAD
    written = [
        pltpu.make_async_copy(
            obuf.at[:, :, pl.ds(h * span, span)], o_hbm.at[:, :, pl.ds(h * span, span)], osem.at[h]
        )
        for h in range(heads)
    ]
    together = 4 if nq % 4 == 0 else 1
    for h in range(heads):
        for k in reversed(order):
            came_r(k, h).wait_recv()
            share_r(k, h).start()
        for k in reversed(order):
            heard_r(k, h).wait_recv()

        def several(i, _):
            for j in range(together):
                far(h, i * together + j)
            return 0

        lax.fori_loop(0, nq // together, several, 0)
        written[h].start()

    for copy in written:
        copy.wait()

    @pl.when(me == 0)
    def _():
        jump_g.wait_send()

    @pl.when(passes | ((me == 0) & (middle > 1)))
    def _():
        send_g.wait_send()

    @pl.when(me < n - 1)
    def _():
        send_w.wait_send()

    @pl.when(me > 0)
    def _():
        share_g.wait_send()
        share_w.wait_send()

    for k in order:
        for h in range(heads):
            send_r(k, h).wait_send()
            share_r(k, h).wait_send()


def body(queries, cache_kv, cache_scale, prompt_key_value, prompt_scale, rand_blocks):
    n = lax.axis_size("ctx")
    nq, rows, width = queries.shape
    nc, block, kvw = cache_kv.shape
    rand = rand_blocks.shape[1]
    cap = max(2, (nq * rand + n - 1) // n)
    heads = kvw // (2 * HEAD)
    lanes = width // (heads * HEAD) * rows
    half = block // 2
    bf, f32 = jnp.bfloat16, jnp.float32
    hbm = pl.BlockSpec(memory_space=pl.ANY)
    dma = pltpu.SemaphoreType.DMA
    grid = (n - 1, heads)
    keys = (NG + rand + WIN + 1) * block
    return pl.pallas_call(
        functools.partial(kernel, n, cap),
        out_shape=jax.ShapeDtypeStruct(queries.shape, bf),
        in_specs=[hbm] * 6,
        out_specs=hbm,
        scratch_shapes=[
            pltpu.VMEM((nq, rows, width), bf),
            pltpu.VMEM((nc, block, kvw), bf),
            pltpu.VMEM((WIN + nq, block, kvw), bf),
            pltpu.VMEM((NG, block, kvw), bf),
            [pltpu.VMEM((n * 2 * cap, half, 2 * HEAD), bf)] * heads,
            pltpu.VMEM((n - 1, heads, cap, half, 2 * HEAD), bf),
            pltpu.VMEM((nq, rows, width), bf),
            pltpu.VMEM((nq, heads, HEAD, lanes), f32),
            pltpu.VMEM((nq, heads, 1, lanes), f32),
            pltpu.VMEM((nq, heads, 1, lanes), f32),
            pltpu.VMEM((block, lanes), f32),
            pltpu.SMEM((nq * rand,), jnp.int32),
            pltpu.SMEM(cache_scale.shape[::-1], f32),
            pltpu.SMEM(prompt_scale.shape[::-1], f32),
            pltpu.SMEM(rand_blocks.shape[::-1], jnp.int32),
            dma((7,)), dma((heads,)),
            dma(grid), dma(grid), dma(grid), dma(grid),
            dma((2,)), dma, dma, dma, dma, dma, dma, dma,
        ],
        compiler_params=pltpu.CompilerParams(
            collective_id=0, has_side_effects=True, vmem_limit_bytes=56 * 2**20
        ),
        cost_estimate=pl.CostEstimate(
            flops=4 * nq * width * rows * keys,
            bytes_accessed=2 * nc * block * kvw + 4 * nq * rows * width,
            transcendentals=nq * heads * lanes * keys,
        ),
    )(queries, cache_kv, cache_scale.T, prompt_key_value, prompt_scale.T, rand_blocks.T)


def solution(mesh):
    in_specs = (
        P(("group", "ctx"), "sub", "kvh"),
        P(("group", "ctx"), None, "kvh"),
        P("group", "kvh"),
        P(("group", "ctx"), None, "kvh"),
        P("group", "kvh"),
        P("group", None),
    )
    out_specs = P(("group", "ctx"), "sub", "kvh")
    return jax.shard_map(body, mesh=mesh, in_specs=in_specs, out_specs=out_specs, check_vma=False)
```
